512 devices in a mesh: ens: 16 (over y, z_hi), sp: 32 (over x, z_lo, core).
Axes of the slice: x: 4, y: 4, z: 16 (z_hi: 4, z_lo: 4; z = z_hi * 4 + z_lo), core: 2. Of those that a mesh axis runs over, the one named last changes fastest.
Arguments:
- embedding: bfloat16 [16, 192, 384, 256], P('ens', 'sp'), may hold values from -6 to 6
- target: bfloat16 [24, 192, 384], P(None, 'sp'), may hold values from -6 to 6
- gain: float32 [256], replicated, may hold values from 0.5 to 1.5
- head_w: bfloat16 [256, 24], replicated, may hold values from -0.375 to 0.375
Outputs:
- grad_head_w: float32 [256, 24], replicated
- grad_gain: float32 [256], replicated
The draws below stay inside these ranges and needn't reach their ends.
All inputs are finite; a program needn't handle non-finite values.
Results may differ from the reference program's by a relative error of at most 0.0049.
The reference program's roundings to bfloat16 on the way count: a program that leaves them out, or rounds other values in their place, can miss the bound.
Values sent between devices are 32-bit elements; how exact they have to be, the bound alone decides.
A program may use at most 64 MiB of HBM per device.

```python
import math
import jax
import jax.numpy as jnp
from jax import lax

EMBED_CHANNELS = 256
NVAR = 24
LATITUDE_ROWS = 192
LONGITUDE_COLUMNS = 384
MMAX = 192
LMAX = 192
MEMBERS = 16


def steps_of(own_key, extent, split, smallest, top_value):
    factor_of, own = 1.0, jax.random.fold_in(own_key, 6)
    for axis_at, shards_of in split:
        draws = jnp.exp(jax.random.uniform(jax.random.fold_in(own, axis_at), (shards_of,), jnp.float32, smallest / len(split), top_value / len(split)))
        factor_of = factor_of * jnp.repeat(draws, extent[axis_at] // shards_of).reshape([-1 if axis == axis_at else 1 for axis in range(len(extent))])
    return factor_of


def bell_draw(rng, dims, width, reach, shards=(), kind=jnp.bfloat16):
    values = width * jax.random.normal(rng, dims, jnp.float32)
    if shards:
        values = values * steps_of(rng, dims, shards, -0.22, 0.18)
    return jnp.clip(values, -reach, reach).astype(kind)


def setup_inputs(seed: int = 0) -> dict:
    keys = jax.random.split(jax.random.key(seed), 5)
    embedding = bell_draw(keys[0], (MEMBERS, LATITUDE_ROWS, LONGITUDE_COLUMNS, EMBED_CHANNELS), 1.0, 6.0, ((0, 16), (1, 32)))
    target = bell_draw(keys[1], (NVAR, LATITUDE_ROWS, LONGITUDE_COLUMNS), 1.0, 6.0, ((1, 32),))
    gain = jnp.clip(1.0 + 0.1 * jax.random.normal(keys[2], (EMBED_CHANNELS,), jnp.float32), 0.5, 1.5)
    head_w = bell_draw(keys[3], (EMBED_CHANNELS, NVAR), EMBED_CHANNELS ** -0.5, 0.375)
    return dict(embedding=embedding, target=target, gain=gain, head_w=head_w)


def dft_table():
    column = jnp.arange(LONGITUDE_COLUMNS, dtype=jnp.int32)
    wave = jnp.arange(MMAX, dtype=jnp.int32)
    phase = column[:, None] * wave[None, :] % LONGITUDE_COLUMNS
    angle = phase.astype(jnp.float32) * (2.0 * math.pi / LONGITUDE_COLUMNS)
    factor = 2.0 * math.pi / LONGITUDE_COLUMNS
    return (jnp.stack([jnp.cos(angle), -jnp.sin(angle)], axis=2) * factor).reshape(LONGITUDE_COLUMNS, 2 * MMAX)

def legendre_rows(m_first, count):
    rows = jnp.arange(LATITUDE_ROWS, dtype=jnp.int32).astype(jnp.float32)
    theta = math.pi * (rows + 0.5) / LATITUDE_ROWS
    cosine = jnp.cos(theta)
    sine = jnp.sin(theta)
    steps_q = jnp.arange(1, MMAX, dtype=jnp.int32).astype(jnp.float32)
    terms = jnp.log((2.0 * steps_q - 1.0) / (2.0 * steps_q))
    running = jnp.concatenate([jnp.zeros((1,), jnp.float32), jnp.cumsum(terms)])
    partial_sum = lax.dynamic_slice_in_dim(running, m_first, count)
    waves = (m_first + jnp.arange(count, dtype=jnp.int32)).astype(jnp.float32)[:, None]
    diagonal = jnp.exp(0.5 * jnp.log((2.0 * waves + 1.0) / (4.0 * math.pi)) + 0.5 * partial_sum[:, None] + waves * jnp.log(sine)[None, :])
    weight = math.pi / LATITUDE_ROWS * sine * math.sqrt(LATITUDE_ROWS * LONGITUDE_COLUMNS / (4.0 * math.pi))

    def advance(carry, degree):
        prev, before = carry
        deg = degree.astype(jnp.float32)
        first = jnp.sqrt((4.0 * deg * deg - 1.0) / jnp.maximum(deg * deg - waves * waves, 1.0))
        second = jnp.sqrt(jnp.maximum((deg - 1.0) ** 2 - waves * waves, 0.0) / jnp.maximum(4.0 * (deg - 1.0) ** 2 - 1.0, 1.0))
        recur = first * (cosine[None, :] * prev - second * before)
        fresh = jnp.where(deg < waves, 0.0, jnp.where(deg == waves, diagonal, recur))
        return ((fresh, prev), fresh * weight[None, :])
    start = jnp.zeros((count, LATITUDE_ROWS), jnp.float32)
    _, table = lax.scan(advance, (start, start), jnp.arange(LMAX, dtype=jnp.int32))
    return table

def apply_layer_norm(flat, gain):
    values = flat.astype(jnp.float32)
    mean_removed = values - lax.optimization_barrier(jnp.mean(values, axis=-1, keepdims=True))
    standardized_input = mean_removed * lax.rsqrt(lax.optimization_barrier(jnp.mean(mean_removed * mean_removed, axis=-1, keepdims=True)) + 1e-05)
    return (standardized_input, (standardized_input * gain[None, :]).astype(jnp.bfloat16))

def slope(diff):
    return diff / jnp.sqrt(diff * diff + 0.01)

def reference(embedding, target, gain, head_w):
    table = dft_table()
    basis = legendre_rows(0, MMAX)
    highest = lax.Precision.HIGHEST

    def to_coef(field):
        four = jnp.dot(field.reshape(NVAR * LATITUDE_ROWS, LONGITUDE_COLUMNS), table, precision=highest, preferred_element_type=jnp.float32)
        four = four.reshape(NVAR, LATITUDE_ROWS, MMAX, 2)
        return jnp.einsum('lmj,vjmp->vmpl', basis, four, precision=highest)

    def member_coef(ensemble_member):
        _, normalized_input = apply_layer_norm(ensemble_member.reshape(LATITUDE_ROWS * LONGITUDE_COLUMNS, EMBED_CHANNELS), gain)
        pred = lax.dot_general(head_w, normalized_input, (((0,), (1,)), ((), ())), preferred_element_type=jnp.float32)
        return to_coef(pred)
    coefs = lax.map(member_coef, embedding)
    truth = to_coef(target.astype(jnp.float32))

    def add_member(index, total):
        other = lax.dynamic_index_in_dim(coefs, index, 0, keepdims=True)
        return total + slope(coefs - other)
    pair = lax.fori_loop(0, MEMBERS, add_member, jnp.zeros_like(coefs))
    gcoef = (slope(coefs - truth[None]) / MEMBERS - pair / (MEMBERS * (MEMBERS - 1))) / LMAX

    def member_grad(carry, inputs):
        ensemble_member, grad_member = inputs
        gfour = jnp.einsum('lmj,vmpl->vjmp', basis, grad_member, precision=highest).reshape(NVAR * LATITUDE_ROWS, 2 * MMAX)
        gpred = jnp.dot(gfour, table.T, precision=highest, preferred_element_type=jnp.float32)
        gpred = gpred.astype(jnp.bfloat16).reshape(NVAR, LATITUDE_ROWS * LONGITUDE_COLUMNS)
        standardized_input, normalized_input = apply_layer_norm(ensemble_member.reshape(LATITUDE_ROWS * LONGITUDE_COLUMNS, EMBED_CHANNELS), gain)
        dweight = lax.dot_general(normalized_input, gpred, (((0,), (1,)), ((), ())), preferred_element_type=jnp.float32)
        normalized_gradient = lax.dot_general(gpred, head_w, (((0,), (1,)), ((), ())), preferred_element_type=jnp.float32)
        gain_gradient = lax.optimization_barrier(jnp.sum(normalized_gradient * standardized_input, axis=0))
        return ((carry[0] + dweight, carry[1] + gain_gradient), None)
    init = (jnp.zeros((EMBED_CHANNELS, NVAR), jnp.float32), jnp.zeros((EMBED_CHANNELS,), jnp.float32))
    (grad_head_w, grad_gain), _ = lax.scan(member_grad, init, (embedding, gcoef))
    return (grad_head_w, grad_gain)
```

```python
import functools
import math

import jax
import jax.numpy as jnp
import ml_dtypes
import numpy as np
from jax import lax
from jax.experimental import pallas as pl
from jax.experimental.pallas import tpu as pltpu
from jax.sharding import PartitionSpec as P

EMBED = 256
NVAR = 24
ROWS = 192
COLS = 384
MMAX = 192
LMAX = 192
MEMBERS = 16
SP = 32
LOCAL_ROWS = ROWS // SP
POINTS = LOCAL_ROWS * COLS
PAIRS = 3
MESH = pl.DeviceIdType.MESH
F32 = jnp.float32
BF16 = jnp.bfloat16


def split_np(x):
    hi = x.astype(np.float32).astype(ml_dtypes.bfloat16)
    lo = (x - hi.astype(np.float64)).astype(np.float32).astype(ml_dtypes.bfloat16)
    return np.stack([hi, lo])


def pair_waves():
    q = (np.arange(PAIRS)[:, None] * SP + np.arange(SP)[None, :])
    return np.stack([q, MMAX - 1 - q])


def dft_tables():
    waves = pair_waves().reshape(2, PAIRS * SP)
    phase = (waves[:, :, None] * np.arange(COLS)[None, None, :]) % COLS
    angle = phase * (2.0 * math.pi / COLS)
    factor = 2.0 * math.pi / COLS
    table = np.stack([np.cos(angle), -np.sin(angle)], axis=1) * factor
    forward = table.reshape(4 * PAIRS * SP, COLS)
    back = np.zeros((4, 128, COLS))
    back[:, : PAIRS * SP] = table.reshape(4, PAIRS * SP, COLS)
    return split_np(forward), split_np(back.reshape(512, COLS))


def legendre_basis():
    theta = math.pi * (np.arange(ROWS) + 0.5) / ROWS
    x, sine = np.cos(theta), np.sin(theta)
    m = np.arange(MMAX, dtype=np.float64)[:, None]
    q = np.arange(1, MMAX, dtype=np.float64)
    running = np.concatenate([[0.0], np.cumsum(np.log((2 * q - 1) / (2 * q)))])[:, None]
    diagonal = np.exp(
        0.5 * np.log((2 * m + 1) / (4 * math.pi)) + 0.5 * running + m * np.log(sine)[None, :]
    )
    weight = math.pi / ROWS * sine * math.sqrt(ROWS * COLS / (4 * math.pi))
    out = np.zeros((LMAX, MMAX, ROWS))
    prev, before = np.zeros((MMAX, ROWS)), np.zeros((MMAX, ROWS))
    for l in range(LMAX):
        a = np.sqrt((4.0 * l * l - 1.0) / np.maximum(l * l - m * m, 1.0)) if l else np.zeros_like(m)
        b = np.sqrt(
            np.maximum((l - 1.0) ** 2 - m * m, 0.0) / np.maximum(4.0 * (l - 1.0) ** 2 - 1.0, 1.0)
        )
        fresh = np.where(l < m, 0.0, np.where(l == m, diagonal, a * (x[None] * prev - b * before)))
        out[l] = fresh * weight[None]
        prev, before = fresh, prev
    return out


def legendre_table():
    basis = legendre_basis()
    table = np.zeros((SP, PAIRS, 256, SP, 8))
    for s in range(SP):
        for i in range(PAIRS):
            q = SP * i + s
            first = basis[q:, q].reshape(-1, SP, LOCAL_ROWS)
            second = basis[MMAX - 1 - q :, MMAX - 1 - q].reshape(-1, SP, LOCAL_ROWS)
            table[s, i, : MMAX - q, :, :LOCAL_ROWS] = first
            table[s, i, MMAX - q : MMAX + 1, :, :LOCAL_ROWS] = second
    both = split_np(table.reshape(SP, PAIRS, 256, 256))
    return np.ascontiguousarray(np.moveaxis(both, 0, 2))


def split(x):
    hi = x.astype(BF16)
    return hi, (x - hi.astype(F32)).astype(BF16)


def dot(a, b):
    return jnp.dot(a, b, preferred_element_type=F32)


def dot_t(a, b):
    return lax.dot_general(a, b, (((1,), (1,)), ((), ())), preferred_element_type=F32)


def three(product, a, b):
    return product(a[0], b[0]) + (product(a[1], b[0]) + product(a[0], b[1]))


def slope(diff):
    return diff * lax.rsqrt(diff * diff + 0.01)


def standardize(values):
    centred = values - jnp.mean(values, axis=-1, keepdims=True)
    return centred * lax.rsqrt(jnp.mean(centred * centred, axis=-1, keepdims=True) + 1e-05)


def kernel(
    emb_hbm, target_ref, gain_ref, head_ref, fwd_ref, back_ref, leg_hbm,
    out_ref,
    emb_ref, leg_ref, feat_ref, target_rows, grid_ref, waves_ref,
    tsend, trecv, psend, precv, csend, crecv, ctruth, gsend, grecv, bsend, brecv,
    rsend, rrecv, esend, erecv,
    load_sem, send_sem, recv_sem,
):
    e = lax.axis_index("ens")
    s = lax.axis_index("sp")
    barrier = pltpu.get_barrier_semaphore()

    def greet_sp(d, carry):
        pl.semaphore_signal(barrier, inc=1, device_id=(e, (s + d) % SP), device_id_type=MESH)
        return carry

    def greet_ens(d, carry):
        pl.semaphore_signal(barrier, inc=1, device_id=((e + d) % MEMBERS, s), device_id_type=MESH)
        return carry

    emb_copy = pltpu.make_async_copy(emb_hbm, emb_ref, load_sem.at[0])
    emb_copy.start()
    leg_copy = pltpu.make_async_copy(leg_hbm.at[s], leg_ref, load_sem.at[1])
    leg_copy.start()
    lax.fori_loop(1, SP, greet_sp, 0)
    lax.fori_loop(1, MEMBERS, greet_ens, 0)

    lane = lax.broadcasted_iota(jnp.int32, (1, 128), 1)
    wide_lane = lax.broadcasted_iota(jnp.int32, (1, 256), 1)

    def waves_to_blocks(target_block):
        field = split(grid_ref[...])
        table = (fwd_ref[0], fwd_ref[1])
        waves_ref[...] = three(dot_t, table, field)
        for row in range(LOCAL_ROWS):
            group, start = (0, 24 * row) if row < 5 else (1, 0)
            parts = [
                pltpu.roll(
                    waves_ref[96 * hp : 96 * hp + 96, 128 * group : 128 * group + 128],
                    (24 * hp - start) % 128, 1,
                )
                for hp in range(4)
            ]
            block = jnp.where(
                lane < 48,
                jnp.where(lane < 24, parts[0], parts[1]),
                jnp.where(lane < 72, parts[2], parts[3]),
            )
            for i in range(PAIRS):
                target_block[i, pl.ds(row, SP, stride=8), :] = block[SP * i : SP * i + SP]

    def exchange_sp(source, dest, at):
        def send(d, carry):
            to = (s + d) % SP
            pltpu.make_async_remote_copy(
                src_ref=source.at[:, pl.ds(pl.multiple_of(8 * to, 8), 8), :],
                dst_ref=dest.at[:, pl.ds(pl.multiple_of(8 * s, 8), 8), :],
                send_sem=send_sem.at[at], recv_sem=recv_sem.at[at],
                device_id=(e, to), device_id_type=MESH,
            ).start()
            return carry

        lax.fori_loop(1, SP, send, 0)
        mine = pl.ds(pl.multiple_of(8 * s, 8), 8)
        dest[:, mine, :] = source[:, mine, :]

    def exchange_ens(source, dest, at):
        def send(d, carry):
            to = (e + d) % MEMBERS
            pltpu.make_async_remote_copy(
                src_ref=source.at[to], dst_ref=dest.at[e],
                send_sem=send_sem.at[at], recv_sem=recv_sem.at[at],
                device_id=(to, s), device_id_type=MESH,
            ).start()
            return carry

        lax.fori_loop(1, MEMBERS, send, 0)
        dest[e] = source[e]

    def settle(piece, sem):
        pltpu.make_async_copy(piece, piece, sem).wait()

    def sp_piece(ref):
        return ref.at[:, pl.ds(0, 8 * (SP - 1)), :]

    def ens_piece(ref):
        return ref.at[pl.ds(0, MEMBERS - 1)]

    pad = jnp.zeros((PAIRS, 256, 128), F32)
    tsend[...] = pad
    psend[...] = pad
    grid_ref[...] = jnp.zeros((256, COLS), F32)
    for v in range(NVAR):
        for c in range(3):
            target_rows[c, 8 * v : 8 * v + LOCAL_ROWS, :] = target_ref[
                v, :, 128 * c : 128 * c + 128
            ].astype(F32)
    for row in range(LOCAL_ROWS):
        at = 24 * row if row < 5 else 128
        for c in range(3):
            grid_ref[at : at + 24, 128 * c : 128 * c + 128] = target_rows[
                c, pl.ds(row, NVAR, stride=8), :
            ]
    waves_to_blocks(tsend)
    pl.semaphore_wait(barrier, SP - 1 + MEMBERS - 1)
    exchange_sp(tsend, trecv, 0)

    emb_copy.wait()
    head_t = head_ref[...].astype(F32).T
    head_t16 = head_t.astype(BF16)
    gain = gain_ref[...]
    step = 64

    def norm_chunk(at, carry):
        rows = pl.ds(pl.multiple_of(at * step, step), step)
        xhat = standardize(emb_ref[rows, :].astype(F32))
        feat_ref[rows, 0:256] = (xhat * gain).astype(BF16)
        return carry

    lax.fori_loop(0, POINTS // step, norm_chunk, 0)
    for row in range(LOCAL_ROWS):
        at = 24 * row if row < 5 else 128
        grid_ref[at : at + 24, :] = dot_t(head_t16, feat_ref[COLS * row : COLS * row + COLS, 0:256])
    waves_to_blocks(psend)
    exchange_sp(psend, precv, 1)

    def xhat_chunk(at, carry):
        rows = pl.ds(pl.multiple_of(at * step, step), step)
        hi, lo = split(standardize(emb_ref[rows, :].astype(F32)))
        feat_ref[rows, 256:512] = hi
        feat_ref[rows, 512:768] = lo
        return carry

    lax.fori_loop(0, POINTS // step, xhat_chunk, 0)
    leg_copy.wait()

    def to_coefficients(received, slices):
        tails = []
        for i in range(PAIRS):
            basis = (leg_ref[i, 0], leg_ref[i, 1])
            terms = three(dot, basis, split(received[i])).T
            edge = MMAX - (SP * i + s)
            packed = jnp.where(wide_lane < edge, terms[0:48], terms[48:96])
            for b in range(3):
                slices[3 * i + b] = packed[16 * b : 16 * b + 16, 0:128]
            tails.append(packed[:, 128:256])
        group3 = jnp.where(lane < 65, tails[0], pltpu.roll(tails[1], 65, 1))
        group4 = jnp.where(
            lane < 65, tails[2], jnp.where(lane < 67, pltpu.roll(tails[1], 2, 1), 0.0)
        )
        for b in range(3):
            slices[9 + b] = group3[16 * b : 16 * b + 16]
            slices[12 + b] = group4[16 * b : 16 * b + 16]
        slices[15] = jnp.zeros((16, 128), F32)

    settle(sp_piece(trecv), recv_sem.at[0])
    to_coefficients(trecv, ctruth)
    settle(sp_piece(precv), recv_sem.at[1])
    to_coefficients(precv, csend)
    exchange_ens(csend, crecv, 2)
    truth = ctruth[e]
    settle(ens_piece(crecv), recv_sem.at[2])

    members = crecv[...]

    def turned(x, by):
        by = by % MEMBERS
        return jnp.concatenate([x[MEMBERS - by :], x[: MEMBERS - by]], axis=0)

    pair = slope(members - turned(members, 8))
    for by in range(1, 8):
        term = slope(members - turned(members, by))
        pair = pair + (term - turned(term, -by))
    gsend[...] = slope(members - truth[None]) * (1.0 / (MEMBERS * LMAX)) - pair * (
        1.0 / (MEMBERS * (MEMBERS - 1) * LMAX)
    )
    exchange_ens(gsend, grecv, 3)
    settle(ens_piece(grecv), recv_sem.at[3])

    groups = [
        jnp.concatenate([grecv[3 * c + b] for b in range(3)], axis=0) for c in range(5)
    ]
    tails = [
        jnp.where(lane < 65, groups[3], 0.0),
        jnp.where(
            lane < 63,
            pltpu.roll(groups[3], 63, 1),
            jnp.where(lane < 65, pltpu.roll(groups[4], 126, 1), 0.0),
        ),
        jnp.where(lane < 65, groups[4], 0.0),
    ]
    for i in range(PAIRS):
        packed = jnp.concatenate([groups[i], tails[i]], axis=1)
        edge = MMAX - (SP * i + s)
        both = jnp.concatenate(
            [
                jnp.where(wide_lane < edge, packed, 0.0),
                jnp.where(wide_lane < edge, 0.0, packed),
                jnp.zeros((32, 256), F32),
            ],
            axis=0,
        )
        basis = (leg_ref[i, 0], leg_ref[i, 1])
        bsend[i] = three(dot, split(both), basis).T
    exchange_sp(bsend, brecv, 4)
    settle(sp_piece(brecv), recv_sem.at[4])

    pieces = []
    for row in range(LOCAL_ROWS):
        block = jnp.concatenate(
            [brecv[i, pl.ds(row, SP, stride=8), :] for i in range(PAIRS)]
            + [jnp.zeros((32, 128), F32)],
            axis=0,
        ).T
        pieces.append(
            jnp.concatenate([block[24 * hp : 24 * hp + 24] for hp in range(4)], axis=1)
        )
    waves = jnp.concatenate(pieces, axis=0)
    table = (back_ref[0], back_ref[1])
    gpred = three(dot, split(waves), table)
    flat = jnp.concatenate(
        [gpred[24 * row : 24 * row + 24] for row in range(LOCAL_ROWS)], axis=1
    ).astype(BF16)
    grads = dot(flat, feat_ref[...])
    gain_grad = jnp.sum(
        (grads[:, 256:512] + grads[:, 512:768]) * head_t, axis=0, keepdims=True
    )
    for v in range(NVAR):
        rsend[v] = grads[v : v + 1, 0:256]
    rsend[NVAR] = gain_grad
    for r in range(NVAR + 1, SP):
        rsend[r] = jnp.zeros((1, 256), F32)

    def scatter(d, carry):
        to = (s + d) % SP
        pltpu.make_async_remote_copy(
            src_ref=rsend.at[to], dst_ref=rrecv.at[s],
            send_sem=send_sem.at[5], recv_sem=recv_sem.at[5],
            device_id=(e, to), device_id_type=MESH,
        ).start()
        return carry

    lax.fori_loop(1, SP, scatter, 0)
    rrecv[s] = rsend[s]
    settle(rrecv.at[pl.ds(0, SP - 1)], recv_sem.at[5])
    total = rrecv[0]
    for r in range(1, SP):
        total = total + rrecv[r]
    esend[...] = total

    def spread(d, carry):
        to = (e + d) % MEMBERS
        pltpu.make_async_remote_copy(
            src_ref=esend, dst_ref=erecv.at[e],
            send_sem=send_sem.at[6], recv_sem=recv_sem.at[6],
            device_id=(to, s), device_id_type=MESH,
        ).start()
        return carry

    lax.fori_loop(1, MEMBERS, spread, 0)
    erecv[e] = total
    settle(erecv.at[pl.ds(0, MEMBERS - 1)], recv_sem.at[6])
    total = erecv[0]
    for r in range(1, MEMBERS):
        total = total + erecv[r]
    out_ref[s] = total

    def gather(d, carry):
        to = (s + d) % SP
        pltpu.make_async_remote_copy(
            src_ref=out_ref.at[s], dst_ref=out_ref.at[s],
            send_sem=send_sem.at[7], recv_sem=recv_sem.at[7],
            device_id=(e, to), device_id_type=MESH,
        ).start()
        return carry

    lax.fori_loop(1, SP, gather, 0)
    settle(out_ref.at[pl.ds(0, SP - 1)], recv_sem.at[7])

    settle(sp_piece(tsend), send_sem.at[0])
    settle(sp_piece(psend), send_sem.at[1])
    settle(ens_piece(csend), send_sem.at[2])
    settle(ens_piece(gsend), send_sem.at[3])
    settle(sp_piece(bsend), send_sem.at[4])
    settle(rsend.at[pl.ds(0, SP - 1)], send_sem.at[5])
    settle(erecv.at[pl.ds(0, MEMBERS - 1)], send_sem.at[6])
    settle(out_ref.at[pl.ds(0, SP - 1)], send_sem.at[7])


def per_device(forward, back, legendre, embedding, target, gain, head_w):
    vmem = pl.BlockSpec(memory_space=pltpu.VMEM)
    anywhere = pl.BlockSpec(memory_space=pl.ANY)
    block = (PAIRS, 256, 128)
    ens_block = (MEMBERS, 16, 128)
    sums = pl.pallas_call(
        kernel,
        out_shape=jax.ShapeDtypeStruct((SP, 1, 256), F32),
        in_specs=[anywhere, vmem, vmem, vmem, vmem, vmem, anywhere],
        out_specs=vmem,
        scratch_shapes=[
            pltpu.VMEM((POINTS, EMBED), BF16),
            pltpu.VMEM((PAIRS, 2, 256, 256), BF16),
            pltpu.VMEM((POINTS, 3 * EMBED), BF16),
            pltpu.VMEM((3, 8 * NVAR, 128), F32),
            pltpu.VMEM((256, COLS), F32),
            pltpu.VMEM((384, 256), F32),
            pltpu.VMEM(block, F32),
            pltpu.VMEM(block, F32),
            pltpu.VMEM(block, F32),
            pltpu.VMEM(block, F32),
            pltpu.VMEM(ens_block, F32),
            pltpu.VMEM(ens_block, F32),
            pltpu.VMEM(ens_block, F32),
            pltpu.VMEM(ens_block, F32),
            pltpu.VMEM(ens_block, F32),
            pltpu.VMEM(block, F32),
            pltpu.VMEM(block, F32),
            pltpu.VMEM((SP, 1, 256), F32),
            pltpu.VMEM((SP, 1, 256), F32),
            pltpu.VMEM((1, 256), F32),
            pltpu.VMEM((MEMBERS, 1, 256), F32),
            pltpu.SemaphoreType.DMA((2,)),
            pltpu.SemaphoreType.DMA((8,)),
            pltpu.SemaphoreType.DMA((8,)),
        ],
        compiler_params=pltpu.CompilerParams(
            collective_id=0, has_side_effects=True, vmem_limit_bytes=40 * 1024 * 1024
        ),
        name="crps",
    )(
        embedding.reshape(POINTS, EMBED), target, gain.reshape(1, EMBED), head_w,
        forward, back, legendre,
    )
    return sums[:NVAR, 0].T, sums[NVAR, 0]


def solution(mesh):
    forward, back = dft_tables()
    legendre = legendre_table()
    in_specs = (P("ens", "sp", None, None), P(None, "sp", None), P(), P())

    def run(*args):
        return jax.shard_map(
            functools.partial(
                per_device, jnp.asarray(forward), jnp.asarray(back), jnp.asarray(legendre)
            ),
            mesh=mesh, in_specs=in_specs, out_specs=(P(), P()), check_vma=False,
        )(*args)

    return run
```

```python
import functools
import math

import jax
import jax.numpy as jnp
import ml_dtypes
import numpy as np
from jax import lax
from jax.experimental import pallas as pl
from jax.experimental.pallas import tpu as pltpu
from jax.sharding import PartitionSpec as P

EMBED = 256
NVAR = 24
ROWS = 192
COLS = 384
MMAX = 192
LMAX = 192
MEMBERS = 16
SP = 32
LOCAL_ROWS = ROWS // SP
POINTS = LOCAL_ROWS * COLS
PAIRS = 3
STEP = 384
MESH = pl.DeviceIdType.MESH
F32 = jnp.float32
BF16 = jnp.bfloat16


def split_np(x):
    hi = x.astype(np.float32).astype(ml_dtypes.bfloat16)
    lo = (x - hi.astype(np.float64)).astype(np.float32).astype(ml_dtypes.bfloat16)
    return np.stack([hi, lo])


def pair_waves():
    q = (np.arange(PAIRS)[:, None] * SP + np.arange(SP)[None, :])
    return np.stack([q, MMAX - 1 - q])


def dft_tables():
    waves = pair_waves().reshape(2, PAIRS * SP)
    phase = (waves[:, :, None] * np.arange(COLS)[None, None, :]) % COLS
    angle = phase * (2.0 * math.pi / COLS)
    factor = 2.0 * math.pi / COLS
    table = np.stack([np.cos(angle), -np.sin(angle)], axis=1) * factor
    forward = table.reshape(4 * PAIRS * SP, COLS)
    back = np.zeros((4, 128, COLS))
    back[:, : PAIRS * SP] = table.reshape(4, PAIRS * SP, COLS)
    return split_np(forward), split_np(back.reshape(512, COLS))


def legendre_basis():
    theta = math.pi * (np.arange(ROWS) + 0.5) / ROWS
    x, sine = np.cos(theta), np.sin(theta)
    m = np.arange(MMAX, dtype=np.float64)[:, None]
    q = np.arange(1, MMAX, dtype=np.float64)
    running = np.concatenate([[0.0], np.cumsum(np.log((2 * q - 1) / (2 * q)))])[:, None]
    diagonal = np.exp(
        0.5 * np.log((2 * m + 1) / (4 * math.pi)) + 0.5 * running + m * np.log(sine)[None, :]
    )
    weight = math.pi / ROWS * sine * math.sqrt(ROWS * COLS / (4 * math.pi))
    out = np.zeros((LMAX, MMAX, ROWS))
    prev, before = np.zeros((MMAX, ROWS)), np.zeros((MMAX, ROWS))
    for l in range(LMAX):
        a = np.sqrt((4.0 * l * l - 1.0) / np.maximum(l * l - m * m, 1.0)) if l else np.zeros_like(m)
        b = np.sqrt(
            np.maximum((l - 1.0) ** 2 - m * m, 0.0) / np.maximum(4.0 * (l - 1.0) ** 2 - 1.0, 1.0)
        )
        fresh = np.where(l < m, 0.0, np.where(l == m, diagonal, a * (x[None] * prev - b * before)))
        out[l] = fresh * weight[None]
        prev, before = fresh, prev
    return out


def legendre_table():
    basis = legendre_basis()
    table = np.zeros((SP, PAIRS, 256, SP, 8))
    for s in range(SP):
        for i in range(PAIRS):
            q = SP * i + s
            first = basis[q:, q].reshape(-1, SP, LOCAL_ROWS)
            second = basis[MMAX - 1 - q :, MMAX - 1 - q].reshape(-1, SP, LOCAL_ROWS)
            table[s, i, : MMAX - q, :, :LOCAL_ROWS] = first
            table[s, i, MMAX - q : MMAX + 1, :, :LOCAL_ROWS] = second
    both = split_np(table.reshape(SP, PAIRS, 256, 256))
    return np.ascontiguousarray(np.moveaxis(both, 0, 2))


def split(x):
    hi = x.astype(BF16)
    return hi, (x - hi.astype(F32)).astype(BF16)


def dot(a, b):
    return jnp.dot(a, b, preferred_element_type=F32)


def dot_t(a, b):
    return lax.dot_general(a, b, (((1,), (1,)), ((), ())), preferred_element_type=F32)


def three(product, a, b):
    return product(a[0], b[0]) + (product(a[1], b[0]) + product(a[0], b[1]))


def slope(diff):
    return diff * lax.rsqrt(diff * diff + 0.01)


def standardize(values):
    centred = values - jnp.mean(values, axis=-1, keepdims=True)
    return centred * lax.rsqrt(jnp.mean(centred * centred, axis=-1, keepdims=True) + 1e-05)


def kernel(
    emb_hbm, target_hbm, gain_hbm, head_hbm, fwd_hbm, back_hbm, leg_hbm,
    out_ref, out_gain_ref,
    emb_ref, target_ref, gain_ref, head_ref, fwd_ref, back_ref, leg_ref,
    feat_ref, grid_ref, waves_ref, third_ref, tall_ref,
    tsend, trecv, psend, precv, csend, crecv, ctruth, gsend, grecv, bsend, brecv,
    rsend, rrecv, esend, erecv, sums_ref,
    load_sem, send_sem, recv_sem,
):
    e = lax.axis_index("ens")
    s = lax.axis_index("sp")
    y, z_hi = e // 4, e % 4
    x, z_lo, core = s // 8, (s // 2) % 4, s % 2
    plane = y * 8 + x * 2 + core
    z = z_hi * 4 + z_lo

    def in_plane(d):
        to = (plane + d) % 32
        return to, ((to // 8) * 4 + z_hi, ((to // 2) % 4) * 8 + z_lo * 2 + to % 2)

    def along_z(d):
        to = (z + d) % 16
        return to, (y * 4 + to // 4, x * 8 + (to % 4) * 2 + core)

    barrier = pltpu.get_barrier_semaphore()

    def greet(device):
        pl.semaphore_signal(barrier, inc=1, device_id=device, device_id_type=MESH)

    def greet_ens(d, carry):
        greet(((e + d) % MEMBERS, s))
        return carry

    def greet_sp(d, carry):
        greet((e, (s + d) % SP))
        return carry

    def greet_z(d, carry):
        greet(
            (
                y * 4 + (z_hi + 1 + d // 3) % 4,
                x * 8 + ((z_lo + 1 + d % 3) % 4) * 2 + core,
            )
        )
        return carry

    def greet_plane(d, carry):
        to = (x * 2 + core + 1 + d % 7) % 8
        greet((((y + 1 + d // 7) % 4) * 4 + z_hi, (to // 2) * 8 + z_lo * 2 + to % 2))
        return carry

    loads = [
        pltpu.make_async_copy(source, dest, load_sem.at[at])
        for at, (source, dest) in enumerate(
            [
                (emb_hbm, emb_ref), (gain_hbm, gain_ref), (head_hbm, head_ref),
                (fwd_hbm, fwd_ref), (target_hbm, target_ref), (leg_hbm.at[s], leg_ref),
                (back_hbm, back_ref),
            ]
        )
    ]
    for load in loads:
        load.start()
    lax.fori_loop(1, MEMBERS, greet_ens, 0)
    lax.fori_loop(0, 9, greet_z, 0)
    lax.fori_loop(1, SP, greet_sp, 0)
    lax.fori_loop(0, 21, greet_plane, 0)

    lane = lax.broadcasted_iota(jnp.int32, (1, 128), 1)
    wide_lane = lax.broadcasted_iota(jnp.int32, (1, 256), 1)

    def turn(value, by):
        by = by % 128
        return pltpu.roll(value, by, 1) if by else value

    def grid_rows(row):
        at = 24 * row if row < 5 else 128
        return slice(at, at + 24)

    def to_waves():
        waves_ref[...] = three(dot_t, (fwd_ref[0], fwd_ref[1]), split(grid_ref[...]))

    def row_waves(row):
        group, start = (0, 24 * row) if row < 5 else (1, 0)
        parts = [
            turn(
                waves_ref[96 * hp : 96 * hp + 96, 128 * group : 128 * group + 128],
                24 * hp - start,
            )
            for hp in range(4)
        ]
        return jnp.where(
            lane < 48,
            jnp.where(lane < 24, parts[0], parts[1]),
            jnp.where(lane < 72, parts[2], parts[3]),
        )

    def every(row):
        return pl.ds(row, SP, stride=8)

    def quarter(row, value):
        return turn(value, 32 * (row % 4) - 64)

    def pack(blocks, buffer):
        rest = [jnp.zeros((SP, 128), F32), jnp.zeros((SP, 128), F32)]
        for row in range(LOCAL_ROWS):
            first, second, third = blocks(row)
            buffer[0, every(row), :] = jnp.where(lane < 96, first, turn(third, 96))
            buffer[1, every(row), :] = jnp.where(lane < 96, second, turn(third, 64))
            at = 32 * (row % 4)
            rest[row // 4] = jnp.where(
                (lane >= at) & (lane < at + 32), quarter(row, third), rest[row // 4]
            )
        buffer[0, every(6), :] = rest[0]
        buffer[0, every(7), :] = rest[1]

    def third_rows(buffer, row):
        return jnp.where(
            lane < 32,
            turn(buffer[0, every(row), :], 32),
            jnp.where(
                lane < 64,
                turn(buffer[1, every(row), :], 64),
                turn(buffer[0, every(6 + row // 4), :], 64 - 32 * (row % 4)),
            ),
        )

    def exchange_sp(source, dest, at):
        def send(d, carry):
            to = (s + d) % SP
            pltpu.make_async_remote_copy(
                src_ref=source.at[:, pl.ds(pl.multiple_of(8 * to, 8), 8), :],
                dst_ref=dest.at[:, pl.ds(pl.multiple_of(8 * s, 8), 8), :],
                send_sem=send_sem.at[at], recv_sem=recv_sem.at[at],
                device_id=(e, to), device_id_type=MESH,
            ).start()
            return carry

        lax.fori_loop(1, SP, send, 0)
        mine = pl.ds(pl.multiple_of(8 * s, 8), 8)
        dest[:, mine, :] = source[:, mine, :]

    def exchange_ens(source, dest, at):
        def send(d, carry):
            to = (e + d) % MEMBERS
            pltpu.make_async_remote_copy(
                src_ref=source.at[to], dst_ref=dest.at[e],
                send_sem=send_sem.at[at], recv_sem=recv_sem.at[at],
                device_id=(to, s), device_id_type=MESH,
            ).start()
            return carry

        lax.fori_loop(1, MEMBERS, send, 0)
        dest[e] = source[e]

    def settle(piece, sem):
        pltpu.make_async_copy(piece, piece, sem).wait()

    def sp_piece(ref):
        return ref.at[:, pl.ds(0, 8 * (SP - 1)), :]

    def ens_piece(ref):
        return ref.at[pl.ds(0, MEMBERS - 1)]

    grid_ref[...] = jnp.zeros((256, COLS), F32)
    psend[...] = jnp.zeros((2, 256, 128), F32)
    tsend[...] = jnp.zeros((1, 256, 128), F32)
    third_ref[...] = jnp.zeros((256, 128), F32)
    for load in loads[:3]:
        load.wait()
    gain = gain_ref[...]
    head = head_ref[...]

    def norm_chunk(at, carry):
        rows = pl.ds(pl.multiple_of(at * STEP, STEP), STEP)
        xhat = standardize(emb_ref[rows, :].astype(F32))
        feat_ref[rows, 0:256] = (xhat * gain).astype(BF16)
        return carry

    lax.fori_loop(0, POINTS // STEP, norm_chunk, 0)
    for row in range(LOCAL_ROWS):
        grid_ref[grid_rows(row), :] = dot_t(head, feat_ref[COLS * row : COLS * row + COLS, 0:256])
    loads[3].wait()
    to_waves()

    def pred_blocks(row):
        block = row_waves(row)
        return [block[SP * i : SP * i + SP] for i in range(PAIRS)]

    pack(pred_blocks, psend)
    pl.semaphore_wait(barrier, SP - 1 + MEMBERS - 1 + 9 + 21)
    exchange_sp(psend, precv, 1)

    loads[4].wait()
    for row in range(LOCAL_ROWS):
        grid_ref[grid_rows(row), :] = target_ref[row].astype(F32)
    to_waves()
    column = (e % 3) * 16
    for row in range(LOCAL_ROWS):
        block = pltpu.roll(row_waves(row), (128 - column) % 128, 1)
        merged = jnp.zeros((SP, 128), F32)
        for i in range(PAIRS):
            part = block[SP * i : SP * i + SP]
            for h in range(2):
                at = 32 * i + 16 * h
                merged = jnp.where(
                    (lane >= at) & (lane < at + 16), turn(part, at - 48 * h), merged
                )
        tsend[0, every(row), :] = merged
    exchange_sp(tsend, trecv, 0)

    def xhat_chunk(at, carry):
        rows = pl.ds(pl.multiple_of(at * STEP, STEP), STEP)
        hi, lo = split(standardize(emb_ref[rows, :].astype(F32)))
        feat_ref[rows, 256:512] = hi
        feat_ref[rows, 512:768] = lo
        return carry

    lax.fori_loop(0, POINTS // STEP, xhat_chunk, 0)
    loads[5].wait()
    loads[6].wait()

    def edge(i):
        return MMAX - (SP * i + s)

    def terms_of(i, fields):
        return three(dot, (leg_ref[i, 0], leg_ref[i, 1]), split(fields)).T

    def tail_groups(tails):
        third = jnp.where(lane < 65, tails[0], pltpu.roll(tails[1], 65, 1))
        fourth = jnp.where(
            lane < 65, tails[2], jnp.where(lane < 67, pltpu.roll(tails[1], 2, 1), 0.0)
        )
        return third, fourth

    settle(sp_piece(precv), recv_sem.at[1])
    for row in range(LOCAL_ROWS):
        third_ref[every(row), :] = third_rows(precv, row)
    tails = []
    for i, fields in enumerate((precv[0], precv[1], third_ref[...])):
        terms = terms_of(i, fields)
        packed = jnp.where(wide_lane < edge(i), terms[0:48], terms[48:96])
        for b in range(3):
            csend[3 * i + b] = packed[16 * b : 16 * b + 16, 0:128]
        tails.append(packed[:, 128:256])
    for c, group in enumerate(tail_groups(tails)):
        for b in range(3):
            csend[9 + 3 * c + b] = group[16 * b : 16 * b + 16]
    csend[15] = jnp.zeros((16, 128), F32)
    exchange_ens(csend, crecv, 2)

    settle(sp_piece(trecv), recv_sem.at[0])
    tails = []
    for i in range(PAIRS):
        terms = terms_of(i, trecv[0])
        packed = jnp.where(
            wide_lane < edge(i), terms[32 * i : 32 * i + 16], terms[32 * i + 16 : 32 * i + 32]
        )
        ctruth[i] = packed[:, 0:128]
        tails.append(packed[:, 128:256])
    ctruth[3], ctruth[4] = tail_groups(tails)
    ctruth[5] = jnp.zeros((16, 128), F32)
    truth = ctruth[e // 3]
    settle(ens_piece(crecv), recv_sem.at[2])

    members = crecv[...]

    def turned(value, by):
        by = by % MEMBERS
        return jnp.concatenate([value[MEMBERS - by :], value[: MEMBERS - by]], axis=0)

    pair = slope(members - turned(members, 8))
    for by in range(1, 8):
        term = slope(members - turned(members, by))
        pair = pair + (term - turned(term, -by))
    gsend[...] = slope(members - truth[None]) * (1.0 / (MEMBERS * LMAX)) - pair * (
        1.0 / (MEMBERS * (MEMBERS - 1) * LMAX)
    )
    exchange_ens(gsend, grecv, 3)
    settle(ens_piece(grecv), recv_sem.at[3])

    groups = [
        jnp.concatenate([grecv[3 * c + b] for b in range(3)], axis=0) for c in range(5)
    ]
    tails = [
        jnp.where(lane < 65, groups[3], 0.0),
        jnp.where(
            lane < 63,
            pltpu.roll(groups[3], 63, 1),
            jnp.where(lane < 65, pltpu.roll(groups[4], 126, 1), 0.0),
        ),
        jnp.where(lane < 65, groups[4], 0.0),
    ]
    for i in range(PAIRS):
        packed = jnp.concatenate([groups[i], tails[i]], axis=1)
        both = jnp.concatenate(
            [
                jnp.where(wide_lane < edge(i), packed, 0.0),
                jnp.where(wide_lane < edge(i), 0.0, packed),
                jnp.zeros((32, 256), F32),
            ],
            axis=0,
        )
        tall_ref[i] = three(dot, split(both), (leg_ref[i, 0], leg_ref[i, 1])).T
    bsend[1] = jnp.zeros((256, 128), F32)
    pack(lambda row: [tall_ref[i, every(row), :] for i in range(PAIRS)], bsend)
    exchange_sp(bsend, brecv, 4)
    settle(sp_piece(brecv), recv_sem.at[4])

    pieces = []
    for row in range(LOCAL_ROWS):
        block = jnp.concatenate(
            [
                brecv[0, every(row), :], brecv[1, every(row), :], third_rows(brecv, row),
                jnp.zeros((32, 128), F32),
            ],
            axis=0,
        ).T
        pieces.append(
            jnp.concatenate([block[24 * hp : 24 * hp + 24] for hp in range(4)], axis=1)
        )
    waves = jnp.concatenate(pieces, axis=0)
    gpred = three(dot, split(waves), (back_ref[0], back_ref[1]))
    flat = jnp.concatenate(
        [gpred[24 * row : 24 * row + 24] for row in range(LOCAL_ROWS)], axis=1
    ).astype(BF16)
    grads = dot(flat, feat_ref[...])
    gain_grad = jnp.sum(
        (grads[:, 256:512] + grads[:, 512:768]) * head.astype(F32), axis=0, keepdims=True
    )
    for v in range(NVAR):
        rsend[v] = grads[v : v + 1, 0:256]
    rsend[NVAR] = gain_grad
    for r in range(NVAR + 1, 32):
        rsend[r] = jnp.zeros((1, 256), F32)

    def scatter(d, carry):
        to, device = in_plane(d)
        pltpu.make_async_remote_copy(
            src_ref=rsend.at[to], dst_ref=rrecv.at[plane],
            send_sem=send_sem.at[5], recv_sem=recv_sem.at[5],
            device_id=device, device_id_type=MESH,
        ).start()
        return carry

    lax.fori_loop(1, 32, scatter, 0)
    rrecv[plane] = rsend[plane]
    settle(rrecv.at[pl.ds(0, 31)], recv_sem.at[5])
    total = rrecv[0]
    for r in range(1, 32):
        total = total + rrecv[r]
    esend[...] = total

    def spread(d, carry):
        _, device = along_z(d)
        pltpu.make_async_remote_copy(
            src_ref=esend, dst_ref=erecv.at[z],
            send_sem=send_sem.at[6], recv_sem=recv_sem.at[6],
            device_id=device, device_id_type=MESH,
        ).start()
        return carry

    lax.fori_loop(1, 16, spread, 0)
    erecv[z] = total
    settle(erecv.at[pl.ds(0, 15)], recv_sem.at[6])
    total = erecv[0]
    for r in range(1, 16):
        total = total + erecv[r]
    sums_ref[plane] = total

    def gather(d, carry):
        _, device = in_plane(d)
        pltpu.make_async_remote_copy(
            src_ref=sums_ref.at[plane], dst_ref=sums_ref.at[plane],
            send_sem=send_sem.at[7], recv_sem=recv_sem.at[7],
            device_id=device, device_id_type=MESH,
        ).start()
        return carry

    lax.fori_loop(1, 32, gather, 0)
    settle(sp_piece(psend), send_sem.at[1])
    settle(sp_piece(tsend), send_sem.at[0])
    settle(ens_piece(csend), send_sem.at[2])
    settle(ens_piece(gsend), send_sem.at[3])
    settle(sp_piece(bsend), send_sem.at[4])
    settle(rsend.at[pl.ds(0, 31)], send_sem.at[5])
    settle(erecv.at[pl.ds(0, 15)], send_sem.at[6])
    settle(sums_ref.at[pl.ds(0, 31)], recv_sem.at[7])
    for v in range(NVAR):
        out_ref[v : v + 1, :] = sums_ref[v]
    out_gain_ref[...] = sums_ref[NVAR]
    settle(sums_ref.at[pl.ds(0, 31)], send_sem.at[7])


def per_device(forward, back, legendre, embedding, target, gain, head_w):
    vmem = pl.BlockSpec(memory_space=pltpu.VMEM)
    hbm = pl.BlockSpec(memory_space=pltpu.HBM)
    ens_block = pltpu.VMEM((MEMBERS, 16, 128), F32)
    two = pltpu.VMEM((2, 256, 128), F32)
    one = pltpu.VMEM((1, 256, 128), F32)
    rows = pltpu.VMEM((32, 1, 256), F32)
    grad_head, grad_gain = pl.pallas_call(
        kernel,
        out_shape=(
            jax.ShapeDtypeStruct((NVAR, EMBED), F32), jax.ShapeDtypeStruct((1, EMBED), F32),
        ),
        in_specs=[hbm] * 7,
        out_specs=(vmem, vmem),
        scratch_shapes=[
            pltpu.VMEM((POINTS, EMBED), BF16),
            pltpu.VMEM((LOCAL_ROWS, NVAR, COLS), BF16),
            pltpu.VMEM((1, EMBED), F32),
            pltpu.VMEM((NVAR, EMBED), BF16),
            pltpu.VMEM((2, 384, COLS), BF16),
            pltpu.VMEM((2, 512, COLS), BF16),
            pltpu.VMEM((PAIRS, 2, 256, 256), BF16),
            pltpu.VMEM((POINTS, 3 * EMBED), BF16),
            pltpu.VMEM((256, COLS), F32),
            pltpu.VMEM((384, 256), F32),
            pltpu.VMEM((256, 128), F32),
            pltpu.VMEM((PAIRS, 256, 128), F32),
            one, one, two, two,
            ens_block, ens_block, pltpu.VMEM((6, 16, 128), F32), ens_block, ens_block,
            two, two,
            rows, rows,
            pltpu.VMEM((1, 256), F32),
            pltpu.VMEM((16, 1, 256), F32),
            rows,
            pltpu.SemaphoreType.DMA((7,)),
            pltpu.SemaphoreType.DMA((8,)),
            pltpu.SemaphoreType.DMA((8,)),
        ],
        compiler_params=pltpu.CompilerParams(
            collective_id=0, has_side_effects=True, vmem_limit_bytes=63 * 1024 * 1024
        ),
        name="crps",
    )(
        embedding.reshape(POINTS, EMBED), jnp.swapaxes(target, 0, 1), gain.reshape(1, EMBED),
        head_w.T, forward, back, legendre,
    )
    return grad_head.T, grad_gain.reshape(EMBED)


def solution(mesh):
    forward, back = dft_tables()
    legendre = legendre_table()
    in_specs = (P("ens", "sp", None, None), P(None, "sp", None), P(), P())

    def run(*args):
        return jax.shard_map(
            functools.partial(
                per_device, jnp.asarray(forward), jnp.asarray(back), jnp.asarray(legendre)
            ),
            mesh=mesh, in_specs=in_specs, out_specs=(P(), P()), check_vma=False,
        )(*args)

    return run
```

```python
import functools
import math

import jax
import jax.numpy as jnp
import ml_dtypes
import numpy as np
from jax import lax
from jax.experimental import pallas as pl
from jax.experimental.pallas import tpu as pltpu
from jax.sharding import PartitionSpec as P

EMBED = 256
NVAR = 24
ROWS = 192
COLS = 384
MMAX = 192
LMAX = 192
MEMBERS = 16
SP = 32
LOCAL_ROWS = ROWS // SP
POINTS = LOCAL_ROWS * COLS
PAIRS = 3
STEP = 384
MESH = pl.DeviceIdType.MESH
F32 = jnp.float32
BF16 = jnp.bfloat16


def split_np(x):
    hi = x.astype(np.float32).astype(ml_dtypes.bfloat16)
    lo = (x - hi.astype(np.float64)).astype(np.float32).astype(ml_dtypes.bfloat16)
    return np.stack([hi, lo])


def pair_waves():
    q = (np.arange(PAIRS)[:, None] * SP + np.arange(SP)[None, :])
    return np.stack([q, MMAX - 1 - q])


def dft_tables():
    waves = pair_waves().reshape(2, PAIRS * SP)
    phase = (waves[:, :, None] * np.arange(COLS)[None, None, :]) % COLS
    angle = phase * (2.0 * math.pi / COLS)
    factor = 2.0 * math.pi / COLS
    table = np.stack([np.cos(angle), -np.sin(angle)], axis=1) * factor
    forward = table.reshape(4 * PAIRS * SP, COLS)
    back = np.zeros((4, 128, COLS))
    back[:, : PAIRS * SP] = table.reshape(4, PAIRS * SP, COLS)
    return split_np(forward), split_np(back.reshape(512, COLS))


def legendre_basis():
    theta = math.pi * (np.arange(ROWS) + 0.5) / ROWS
    x, sine = np.cos(theta), np.sin(theta)
    m = np.arange(MMAX, dtype=np.float64)[:, None]
    q = np.arange(1, MMAX, dtype=np.float64)
    running = np.concatenate([[0.0], np.cumsum(np.log((2 * q - 1) / (2 * q)))])[:, None]
    diagonal = np.exp(
        0.5 * np.log((2 * m + 1) / (4 * math.pi)) + 0.5 * running + m * np.log(sine)[None, :]
    )
    weight = math.pi / ROWS * sine * math.sqrt(ROWS * COLS / (4 * math.pi))
    out = np.zeros((LMAX, MMAX, ROWS))
    prev, before = np.zeros((MMAX, ROWS)), np.zeros((MMAX, ROWS))
    for l in range(LMAX):
        a = np.sqrt((4.0 * l * l - 1.0) / np.maximum(l * l - m * m, 1.0)) if l else np.zeros_like(m)
        b = np.sqrt(
            np.maximum((l - 1.0) ** 2 - m * m, 0.0) / np.maximum(4.0 * (l - 1.0) ** 2 - 1.0, 1.0)
        )
        fresh = np.where(l < m, 0.0, np.where(l == m, diagonal, a * (x[None] * prev - b * before)))
        out[l] = fresh * weight[None]
        prev, before = fresh, prev
    return out


def legendre_table():
    basis = legendre_basis()
    table = np.zeros((SP, PAIRS, 256, SP, 8))
    for s in range(SP):
        for i in range(PAIRS):
            q = SP * i + s
            first = basis[q:, q].reshape(-1, SP, LOCAL_ROWS)
            second = basis[MMAX - 1 - q :, MMAX - 1 - q].reshape(-1, SP, LOCAL_ROWS)
            table[s, i, : MMAX - q, :, :LOCAL_ROWS] = first
            table[s, i, MMAX - q : MMAX + 1, :, :LOCAL_ROWS] = second
    both = split_np(table.reshape(SP, PAIRS, 256, 256))
    return np.ascontiguousarray(np.moveaxis(both, 0, 2))


def split(x):
    hi = x.astype(BF16)
    return hi, (x - hi.astype(F32)).astype(BF16)


def dot(a, b):
    return jnp.dot(a, b, preferred_element_type=F32)


def dot_t(a, b):
    return lax.dot_general(a, b, (((1,), (1,)), ((), ())), preferred_element_type=F32)


def three(product, a, b):
    return product(a[0], b[0]) + (product(a[1], b[0]) + product(a[0], b[1]))


def slope(diff):
    return diff * lax.rsqrt(diff * diff + 0.01)


def standardize(values):
    centred = values - jnp.mean(values, axis=-1, keepdims=True)
    return centred * lax.rsqrt(jnp.mean(centred * centred, axis=-1, keepdims=True) + 1e-05)


def far(n):
    return (2 + n + n // 2 + 2 * (n // 3)) % 4


def copy_kernel(head_in, gain_in, head_out, gain_out, sems):
    copies = [
        pltpu.make_async_copy(head_in, head_out, sems.at[0]),
        pltpu.make_async_copy(gain_in, gain_out, sems.at[1]),
    ]
    for copy in copies:
        copy.start()
    for copy in copies:
        copy.wait()


def kernel(
    emb_hbm, target_hbm, gain_hbm, head_hbm, fwd_hbm, back_hbm, leg_hbm,
    out_ref, out_gain_ref,
    emb_ref, target_ref, gain_ref, head_ref, fwd_ref, back_ref, leg_ref,
    feat_ref, grid_ref, waves_ref, third_ref, tall_ref,
    tsend, trecv, psend, precv, csend, crecv, ctruth, gsend, grecv, bsend, brecv,
    rsend, rrecv, esend, erecv, sums_ref,
    load_sem, send_sem, recv_sem,
):
    e = lax.axis_index("ens")
    s = lax.axis_index("sp")
    y, z_hi = e // 4, e % 4
    x, z_lo, core = s // 8, (s // 2) % 4, s % 2
    plane = y * 8 + x * 2 + core
    z = z_hi * 4 + z_lo

    def in_plane(n):
        to_y, to_x, to_core = (y + far(n // 8)) % 4, (x + far(n % 8 // 2)) % 4, (core + n + 1) % 2
        return to_y * 8 + to_x * 2 + to_core, (to_y * 4 + z_hi, to_x * 8 + z_lo * 2 + to_core)

    def along_z(n):
        to = (z + 8 + (n + 1) // 2 * (1 - 2 * ((n + 1) % 2))) % 16
        return to, (y * 4 + to // 4, x * 8 + to % 4 * 2 + core)

    def in_sp(n):
        to_z, to_x, to_core = (z_lo + far(n // 8)) % 4, (x + far(n % 8 // 2)) % 4, (core + n + 1) % 2
        to = to_x * 8 + to_z * 2 + to_core
        return to, (e, to)

    def in_ens(n):
        to = (y + far(n % 4)) % 4 * 4 + (z_hi + far(n // 4)) % 4
        return to, (to, s)

    barrier = pltpu.get_barrier_semaphore()

    def greet(device):
        pl.semaphore_signal(barrier, inc=1, device_id=device, device_id_type=MESH)

    def greet_ens(n, carry):
        greet(in_ens(n)[1])
        return carry

    def greet_sp(n, carry):
        greet(in_sp(n)[1])
        return carry

    def greet_z(d, carry):
        greet(
            (
                y * 4 + (z_hi + 1 + d // 3) % 4,
                x * 8 + ((z_lo + 1 + d % 3) % 4) * 2 + core,
            )
        )
        return carry

    def greet_plane(d, carry):
        to = (x * 2 + core + 1 + d % 7) % 8
        greet((((y + 1 + d // 7) % 4) * 4 + z_hi, (to // 2) * 8 + z_lo * 2 + to % 2))
        return carry

    loads = [
        pltpu.make_async_copy(source, dest, load_sem.at[at])
        for at, (source, dest) in enumerate(
            [
                (emb_hbm, emb_ref), (gain_hbm, gain_ref), (head_hbm, head_ref),
                (fwd_hbm, fwd_ref), (target_hbm, target_ref), (leg_hbm.at[s], leg_ref),
                (back_hbm, back_ref),
            ]
        )
    ]
    for load in loads:
        load.start()
    lax.fori_loop(0, MEMBERS - 1, greet_ens, 0)
    lax.fori_loop(0, 9, greet_z, 0)
    lax.fori_loop(0, SP - 1, greet_sp, 0)
    lax.fori_loop(0, 21, greet_plane, 0)

    lane = lax.broadcasted_iota(jnp.int32, (1, 128), 1)
    wide_lane = lax.broadcasted_iota(jnp.int32, (1, 256), 1)

    def turn(value, by):
        by = by % 128
        return pltpu.roll(value, by, 1) if by else value

    def grid_rows(row):
        at = 24 * row if row < 5 else 128
        return slice(at, at + 24)

    def to_waves():
        waves_ref[...] = three(dot_t, (fwd_ref[0], fwd_ref[1]), split(grid_ref[...]))

    def row_waves(row):
        group, start = (0, 24 * row) if row < 5 else (1, 0)
        parts = [
            turn(
                waves_ref[96 * hp : 96 * hp + 96, 128 * group : 128 * group + 128],
                24 * hp - start,
            )
            for hp in range(4)
        ]
        return jnp.where(
            lane < 48,
            jnp.where(lane < 24, parts[0], parts[1]),
            jnp.where(lane < 72, parts[2], parts[3]),
        )

    def every(row, block=0):
        return pl.ds(8 * block + row, SP, stride=16)

    def quarter(row, value):
        return turn(value, 32 * (row % 4) - 64)

    def pack(blocks, buffer):
        rest = [jnp.zeros((SP, 128), F32), jnp.zeros((SP, 128), F32)]
        for row in range(LOCAL_ROWS):
            first, second, third = blocks(row)
            buffer[every(row), :] = jnp.where(lane < 96, first, turn(third, 96))
            buffer[every(row, 1), :] = jnp.where(lane < 96, second, turn(third, 64))
            at = 32 * (row % 4)
            rest[row // 4] = jnp.where(
                (lane >= at) & (lane < at + 32), quarter(row, third), rest[row // 4]
            )
        buffer[every(6), :] = rest[0]
        buffer[every(7), :] = rest[1]

    def third_rows(buffer, row):
        return jnp.where(
            lane < 32,
            turn(buffer[every(row), :], 32),
            jnp.where(
                lane < 64,
                turn(buffer[every(row, 1), :], 64),
                turn(buffer[every(6 + row // 4), :], 64 - 32 * (row % 4)),
            ),
        )

    def exchange_sp(source, dest, at):
        size = source.shape[0] // SP

        def place(owner):
            return pl.ds(pl.multiple_of(size * owner, size), size)

        def send(n, carry):
            to, device = in_sp(n)
            pltpu.make_async_remote_copy(
                src_ref=source.at[place(to)],
                dst_ref=dest.at[place(s)],
                send_sem=send_sem.at[at], recv_sem=recv_sem.at[at],
                device_id=device, device_id_type=MESH,
            ).start()
            return carry

        lax.fori_loop(0, SP - 1, send, 0)
        dest[place(s), :] = source[place(s), :]

    def exchange_ens(source, dest, at):
        def send(n, carry):
            to, device = in_ens(n)
            pltpu.make_async_remote_copy(
                src_ref=source.at[to], dst_ref=dest.at[e],
                send_sem=send_sem.at[at], recv_sem=recv_sem.at[at],
                device_id=device, device_id_type=MESH,
            ).start()
            return carry

        lax.fori_loop(0, MEMBERS - 1, send, 0)
        dest[e] = source[e]

    def settle(piece, sem):
        pltpu.make_async_copy(piece, piece, sem).wait()

    def sp_piece(ref):
        return ref.at[pl.ds(0, ref.shape[0] // SP * (SP - 1))]

    def ens_piece(ref):
        return ref.at[pl.ds(0, MEMBERS - 1)]

    grid_ref[...] = jnp.zeros((256, COLS), F32)
    psend[...] = jnp.zeros((512, 128), F32)
    tsend[...] = jnp.zeros((256, 128), F32)
    third_ref[...] = jnp.zeros((256, 128), F32)
    for load in loads[:3]:
        load.wait()
    gain = gain_ref[...]
    head = head_ref[...]

    def norm_chunk(at, carry):
        rows = pl.ds(pl.multiple_of(at * STEP, STEP), STEP)
        xhat = standardize(emb_ref[rows, :].astype(F32))
        feat_ref[rows, 0:256] = (xhat * gain).astype(BF16)
        return carry

    lax.fori_loop(0, POINTS // STEP, norm_chunk, 0)
    for row in range(LOCAL_ROWS):
        grid_ref[grid_rows(row), :] = dot_t(head, feat_ref[COLS * row : COLS * row + COLS, 0:256])
    loads[3].wait()
    to_waves()

    def pred_blocks(row):
        block = row_waves(row)
        return [block[SP * i : SP * i + SP] for i in range(PAIRS)]

    pack(pred_blocks, psend)
    pl.semaphore_wait(barrier, SP - 1 + MEMBERS - 1 + 9 + 21)
    exchange_sp(psend, precv, 1)

    loads[4].wait()
    for row in range(LOCAL_ROWS):
        grid_ref[grid_rows(row), :] = target_ref[row].astype(F32)
    to_waves()
    column = (e % 3) * 16
    for row in range(LOCAL_ROWS):
        block = pltpu.roll(row_waves(row), (128 - column) % 128, 1)
        merged = jnp.zeros((SP, 128), F32)
        for i in range(PAIRS):
            part = block[SP * i : SP * i + SP]
            for h in range(2):
                at = 32 * i + 16 * h
                merged = jnp.where(
                    (lane >= at) & (lane < at + 16), turn(part, at - 48 * h), merged
                )
        tsend[pl.ds(row, SP, stride=8), :] = merged
    exchange_sp(tsend, trecv, 0)

    def xhat_chunk(at, carry):
        rows = pl.ds(pl.multiple_of(at * STEP, STEP), STEP)
        hi, lo = split(standardize(emb_ref[rows, :].astype(F32)))
        feat_ref[rows, 256:512] = hi
        feat_ref[rows, 512:768] = lo
        return carry

    lax.fori_loop(0, POINTS // STEP, xhat_chunk, 0)
    loads[5].wait()
    loads[6].wait()

    def edge(i):
        return MMAX - (SP * i + s)

    def terms_of(i, fields):
        return three(dot, (leg_ref[i, 0], leg_ref[i, 1]), split(fields)).T

    def tail_groups(tails):
        third = jnp.where(lane < 65, tails[0], pltpu.roll(tails[1], 65, 1))
        fourth = jnp.where(
            lane < 65, tails[2], jnp.where(lane < 67, pltpu.roll(tails[1], 2, 1), 0.0)
        )
        return third, fourth

    settle(sp_piece(precv), recv_sem.at[1])
    for row in range(LOCAL_ROWS):
        third_ref[pl.ds(row, SP, stride=8), :] = third_rows(precv, row)
    tails = []
    blocks = precv[...].reshape(SP, 2, 8, 128)
    for i, fields in enumerate(
        (blocks[:, 0].reshape(256, 128), blocks[:, 1].reshape(256, 128), third_ref[...])
    ):
        terms = terms_of(i, fields)
        packed = jnp.where(wide_lane < edge(i), terms[0:48], terms[48:96])
        for b in range(3):
            csend[3 * i + b] = packed[16 * b : 16 * b + 16, 0:128]
        tails.append(packed[:, 128:256])
    for c, group in enumerate(tail_groups(tails)):
        for b in range(3):
            csend[9 + 3 * c + b] = group[16 * b : 16 * b + 16]
    csend[15] = jnp.zeros((16, 128), F32)
    exchange_ens(csend, crecv, 2)

    settle(sp_piece(trecv), recv_sem.at[0])
    tails = []
    for i in range(PAIRS):
        terms = terms_of(i, trecv[...])
        packed = jnp.where(
            wide_lane < edge(i), terms[32 * i : 32 * i + 16], terms[32 * i + 16 : 32 * i + 32]
        )
        ctruth[i] = packed[:, 0:128]
        tails.append(packed[:, 128:256])
    ctruth[3], ctruth[4] = tail_groups(tails)
    ctruth[5] = jnp.zeros((16, 128), F32)
    truth = ctruth[e // 3]
    settle(ens_piece(crecv), recv_sem.at[2])

    members = crecv[...]

    def turned(value, by):
        by = by % MEMBERS
        return jnp.concatenate([value[MEMBERS - by :], value[: MEMBERS - by]], axis=0)

    pair = slope(members - turned(members, 8))
    for by in range(1, 8):
        term = slope(members - turned(members, by))
        pair = pair + (term - turned(term, -by))
    gsend[...] = slope(members - truth[None]) * (1.0 / (MEMBERS * LMAX)) - pair * (
        1.0 / (MEMBERS * (MEMBERS - 1) * LMAX)
    )
    exchange_ens(gsend, grecv, 3)
    settle(ens_piece(grecv), recv_sem.at[3])

    groups = [
        jnp.concatenate([grecv[3 * c + b] for b in range(3)], axis=0) for c in range(5)
    ]
    tails = [
        jnp.where(lane < 65, groups[3], 0.0),
        jnp.where(
            lane < 63,
            pltpu.roll(groups[3], 63, 1),
            jnp.where(lane < 65, pltpu.roll(groups[4], 126, 1), 0.0),
        ),
        jnp.where(lane < 65, groups[4], 0.0),
    ]
    for i in range(PAIRS):
        packed = jnp.concatenate([groups[i], tails[i]], axis=1)
        both = jnp.concatenate(
            [
                jnp.where(wide_lane < edge(i), packed, 0.0),
                jnp.where(wide_lane < edge(i), 0.0, packed),
                jnp.zeros((32, 256), F32),
            ],
            axis=0,
        )
        tall_ref[i] = three(dot, split(both), (leg_ref[i, 0], leg_ref[i, 1])).T
    bsend[...] = jnp.zeros((512, 128), F32)
    pack(lambda row: [tall_ref[i, pl.ds(row, SP, stride=8), :] for i in range(PAIRS)], bsend)
    exchange_sp(bsend, brecv, 4)
    settle(sp_piece(brecv), recv_sem.at[4])

    pieces = []
    for row in range(LOCAL_ROWS):
        block = jnp.concatenate(
            [
                brecv[every(row), :], brecv[every(row, 1), :], third_rows(brecv, row),
                jnp.zeros((32, 128), F32),
            ],
            axis=0,
        ).T
        pieces.append(
            jnp.concatenate([block[24 * hp : 24 * hp + 24] for hp in range(4)], axis=1)
        )
    waves = jnp.concatenate(pieces, axis=0)
    gpred = three(dot, split(waves), (back_ref[0], back_ref[1]))
    flat = jnp.concatenate(
        [gpred[24 * row : 24 * row + 24] for row in range(LOCAL_ROWS)], axis=1
    ).astype(BF16)
    grads = dot(flat, feat_ref[...])
    gain_grad = jnp.sum(
        (grads[:, 256:512] + grads[:, 512:768]) * head.astype(F32), axis=0, keepdims=True
    )
    for v in range(NVAR):
        rsend[v] = grads[v : v + 1, 0:256]
    rsend[NVAR] = gain_grad
    for r in range(NVAR + 1, 32):
        rsend[r] = jnp.zeros((1, 256), F32)

    def scatter(n, carry):
        to, device = in_plane(n)
        pltpu.make_async_remote_copy(
            src_ref=rsend.at[to], dst_ref=rrecv.at[plane],
            send_sem=send_sem.at[5], recv_sem=recv_sem.at[5],
            device_id=device, device_id_type=MESH,
        ).start()
        return carry

    lax.fori_loop(0, 31, scatter, 0)
    rrecv[plane] = rsend[plane]
    settle(rrecv.at[pl.ds(0, 31)], recv_sem.at[5])
    total = rrecv[0]
    for r in range(1, 32):
        total = total + rrecv[r]
    esend[...] = total

    def spread(n, carry):
        _, device = along_z(n)
        pltpu.make_async_remote_copy(
            src_ref=esend, dst_ref=erecv.at[z],
            send_sem=send_sem.at[6], recv_sem=recv_sem.at[6],
            device_id=device, device_id_type=MESH,
        ).start()
        return carry

    lax.fori_loop(0, 15, spread, 0)
    erecv[z] = total
    settle(erecv.at[pl.ds(0, 15)], recv_sem.at[6])
    total = erecv[0]
    for r in range(1, 16):
        total = total + erecv[r]
    sums_ref[plane] = total

    def gather(n, carry):
        _, device = in_plane(n)
        pltpu.make_async_remote_copy(
            src_ref=sums_ref.at[plane], dst_ref=sums_ref.at[plane],
            send_sem=send_sem.at[7], recv_sem=recv_sem.at[7],
            device_id=device, device_id_type=MESH,
        ).start()
        return carry

    lax.fori_loop(0, 31, gather, 0)
    settle(sp_piece(psend), send_sem.at[1])
    settle(sp_piece(tsend), send_sem.at[0])
    settle(ens_piece(csend), send_sem.at[2])
    settle(ens_piece(gsend), send_sem.at[3])
    settle(sp_piece(bsend), send_sem.at[4])
    settle(rsend.at[pl.ds(0, 31)], send_sem.at[5])
    settle(erecv.at[pl.ds(0, 15)], send_sem.at[6])
    settle(sums_ref.at[pl.ds(0, 31)], recv_sem.at[7])
    for v in range(NVAR):
        out_ref[v : v + 1, :] = sums_ref[v]
    out_gain_ref[...] = sums_ref[NVAR]
    settle(sums_ref.at[pl.ds(0, 31)], send_sem.at[7])


def per_device(forward, back, legendre, embedding, target, gain, head_w):
    vmem = pl.BlockSpec(memory_space=pltpu.VMEM)
    hbm = pl.BlockSpec(memory_space=pltpu.HBM)
    ens_block = pltpu.VMEM((MEMBERS, 16, 128), F32)
    two = pltpu.VMEM((512, 128), F32)
    one = pltpu.VMEM((256, 128), F32)
    rows = pltpu.VMEM((32, 1, 256), F32)
    grad_head, grad_gain = pl.pallas_call(
        kernel,
        out_shape=(
            jax.ShapeDtypeStruct((NVAR, EMBED), F32), jax.ShapeDtypeStruct((1, EMBED), F32),
        ),
        in_specs=[hbm] * 7,
        out_specs=(vmem, vmem),
        scratch_shapes=[
            pltpu.VMEM((POINTS, EMBED), BF16),
            pltpu.VMEM((LOCAL_ROWS, NVAR, COLS), BF16),
            pltpu.VMEM((1, EMBED), F32),
            pltpu.VMEM((NVAR, EMBED), BF16),
            pltpu.VMEM((2, 384, COLS), BF16),
            pltpu.VMEM((2, 512, COLS), BF16),
            pltpu.VMEM((PAIRS, 2, 256, 256), BF16),
            pltpu.VMEM((POINTS, 3 * EMBED), BF16),
            pltpu.VMEM((256, COLS), F32),
            pltpu.VMEM((384, 256), F32),
            pltpu.VMEM((256, 128), F32),
            pltpu.VMEM((PAIRS, 256, 128), F32),
            one, one, two, two,
            ens_block, ens_block, pltpu.VMEM((6, 16, 128), F32), ens_block, ens_block,
            two, two,
            rows, rows,
            pltpu.VMEM((1, 256), F32),
            pltpu.VMEM((16, 1, 256), F32),
            rows,
            pltpu.SemaphoreType.DMA((7,)),
            pltpu.SemaphoreType.DMA((8,)),
            pltpu.SemaphoreType.DMA((8,)),
        ],
        compiler_params=pltpu.CompilerParams(
            collective_id=0, has_side_effects=True, vmem_limit_bytes=63 * 1024 * 1024
        ),
        name="crps",
    )(
        embedding.reshape(POINTS, EMBED), jnp.swapaxes(target, 0, 1), gain.reshape(1, EMBED),
        head_w.T, forward, back, legendre,
    )
    grad_head, grad_gain = pl.pallas_call(
        copy_kernel,
        out_shape=(
            jax.ShapeDtypeStruct((NVAR, EMBED), F32), jax.ShapeDtypeStruct((1, EMBED), F32),
        ),
        in_specs=[hbm, hbm],
        out_specs=(hbm, hbm),
        scratch_shapes=[pltpu.SemaphoreType.DMA((2,))],
        compiler_params=pltpu.CompilerParams(vmem_limit_bytes=63 * 1024 * 1024),
        name="results",
    )(grad_head, grad_gain)
    return grad_head.T, grad_gain.reshape(EMBED)


def solution(mesh):
    forward, back = dft_tables()
    legendre = legendre_table()
    in_specs = (P("ens", "sp", None, None), P(None, "sp", None), P(), P())

    def run(*args):
        return jax.shard_map(
            functools.partial(
                per_device, jnp.asarray(forward), jnp.asarray(back), jnp.asarray(legendre)
            ),
            mesh=mesh, in_specs=in_specs, out_specs=(P(), P()), check_vma=False,
        )(*args)

    return run
```

```python
import functools
import math

import jax
import jax.numpy as jnp
import ml_dtypes
import numpy as np
from jax import lax
from jax.experimental import pallas as pl
from jax.experimental.pallas import tpu as pltpu
from jax.sharding import PartitionSpec as P

EMBED = 256
NVAR = 24
ROWS = 192
COLS = 384
MMAX = 192
LMAX = 192
MEMBERS = 16
SP = 32
LOCAL_ROWS = ROWS // SP
POINTS = LOCAL_ROWS * COLS
PAIRS = 3
STEP = 384
MESH = pl.DeviceIdType.MESH
F32 = jnp.float32
BF16 = jnp.bfloat16


def split_np(x):
    hi = x.astype(np.float32).astype(ml_dtypes.bfloat16)
    lo = (x - hi.astype(np.float64)).astype(np.float32).astype(ml_dtypes.bfloat16)
    return np.stack([hi, lo])


def pair_waves():
    q = (np.arange(PAIRS)[:, None] * SP + np.arange(SP)[None, :])
    return np.stack([q, MMAX - 1 - q])


def dft_tables():
    waves = pair_waves().reshape(2, PAIRS * SP)
    phase = (waves[:, :, None] * np.arange(COLS)[None, None, :]) % COLS
    angle = phase * (2.0 * math.pi / COLS)
    factor = 2.0 * math.pi / COLS
    table = np.stack([np.cos(angle), -np.sin(angle)], axis=1) * factor
    forward = table.reshape(4 * PAIRS * SP, COLS)
    back = np.zeros((4, 128, COLS))
    back[:, : PAIRS * SP] = table.reshape(4, PAIRS * SP, COLS)
    return split_np(forward), split_np(back.reshape(512, COLS))


def legendre_basis():
    theta = math.pi * (np.arange(ROWS) + 0.5) / ROWS
    x, sine = np.cos(theta), np.sin(theta)
    m = np.arange(MMAX, dtype=np.float64)[:, None]
    q = np.arange(1, MMAX, dtype=np.float64)
    running = np.concatenate([[0.0], np.cumsum(np.log((2 * q - 1) / (2 * q)))])[:, None]
    diagonal = np.exp(
        0.5 * np.log((2 * m + 1) / (4 * math.pi)) + 0.5 * running + m * np.log(sine)[None, :]
    )
    weight = math.pi / ROWS * sine * math.sqrt(ROWS * COLS / (4 * math.pi))
    out = np.zeros((LMAX, MMAX, ROWS))
    prev, before = np.zeros((MMAX, ROWS)), np.zeros((MMAX, ROWS))
    for l in range(LMAX):
        a = np.sqrt((4.0 * l * l - 1.0) / np.maximum(l * l - m * m, 1.0)) if l else np.zeros_like(m)
        b = np.sqrt(
            np.maximum((l - 1.0) ** 2 - m * m, 0.0) / np.maximum(4.0 * (l - 1.0) ** 2 - 1.0, 1.0)
        )
        fresh = np.where(l < m, 0.0, np.where(l == m, diagonal, a * (x[None] * prev - b * before)))
        out[l] = fresh * weight[None]
        prev, before = fresh, prev
    return out


def legendre_table():
    basis = legendre_basis()
    table = np.zeros((SP, PAIRS, 256, SP, 8))
    for s in range(SP):
        for i in range(PAIRS):
            q = SP * i + s
            first = basis[q:, q].reshape(-1, SP, LOCAL_ROWS)
            second = basis[MMAX - 1 - q :, MMAX - 1 - q].reshape(-1, SP, LOCAL_ROWS)
            table[s, i, : MMAX - q, :, :LOCAL_ROWS] = first
            table[s, i, MMAX - q : MMAX + 1, :, :LOCAL_ROWS] = second
    both = split_np(table.reshape(SP, PAIRS, 256, 256))
    return np.ascontiguousarray(np.moveaxis(both, 0, 2))


def split(x):
    hi = x.astype(BF16)
    return hi, (x - hi.astype(F32)).astype(BF16)


def dot(a, b):
    return jnp.dot(a, b, preferred_element_type=F32)


def dot_t(a, b):
    return lax.dot_general(a, b, (((1,), (1,)), ((), ())), preferred_element_type=F32)


def three(product, a, b):
    return product(a[0], b[0]) + (product(a[1], b[0]) + product(a[0], b[1]))


def slope(diff):
    return diff * lax.rsqrt(diff * diff + 0.01)


def standardize(values):
    centred = values - jnp.mean(values, axis=-1, keepdims=True)
    return centred * lax.rsqrt(jnp.mean(centred * centred, axis=-1, keepdims=True) + 1e-05)


def far(n):
    return (2 + n + n // 2 + 2 * (n // 3)) % 4


def copy_kernel(head_in, gain_in, head_out, gain_out, sems):
    copies = [
        pltpu.make_async_copy(head_in, head_out, sems.at[0]),
        pltpu.make_async_copy(gain_in, gain_out, sems.at[1]),
    ]
    for copy in copies:
        copy.start()
    for copy in copies:
        copy.wait()


def kernel(
    emb_hbm, target_hbm, gain_hbm, head_hbm, fwd_hbm, back_hbm, leg_hbm,
    out_ref, out_gain_ref,
    emb_ref, target_ref, gain_ref, head_ref, fwd_ref, back_ref, leg_ref,
    feat_ref, grid_ref, waves_ref, third_ref, tall_ref,
    tsend, trecv, psend, precv, csend, crecv, ctruth, gsend, grecv, bsend, brecv,
    rsend, rrecv, esend, erecv, sums_ref,
    load_sem, send_sem, recv_sem,
):
    e = lax.axis_index("ens")
    s = lax.axis_index("sp")
    y, z_hi = e // 4, e % 4
    x, z_lo, core = s // 8, (s // 2) % 4, s % 2
    plane = y * 8 + x * 2 + core
    z = z_hi * 4 + z_lo

    def in_plane(n):
        to_y, to_x, to_core = (y + far(n // 8)) % 4, (x + far(n % 8 // 2)) % 4, (core + n + 1) % 2
        return to_y * 8 + to_x * 2 + to_core, (to_y * 4 + z_hi, to_x * 8 + z_lo * 2 + to_core)

    def along_z(n):
        to = (z + 8 + (n + 1) // 2 * (1 - 2 * ((n + 1) % 2))) % 16
        return to, (y * 4 + to // 4, x * 8 + to % 4 * 2 + core)

    def in_sp(n):
        to_z, to_x, to_core = (z_lo + far(n // 8)) % 4, (x + far(n % 8 // 2)) % 4, (core + n + 1) % 2
        to = to_x * 8 + to_z * 2 + to_core
        return to, (e, to)

    def in_ens(n):
        to = (y + far(n % 4)) % 4 * 4 + (z_hi + far(n // 4)) % 4
        return to, (to, s)

    barrier = pltpu.get_barrier_semaphore()

    def greet(device):
        pl.semaphore_signal(barrier, inc=1, device_id=device, device_id_type=MESH)

    def greet_ens(n, carry):
        greet(in_ens(n)[1])
        return carry

    def greet_sp(n, carry):
        greet(in_sp(n)[1])
        return carry

    def greet_z(d, carry):
        greet(
            (
                y * 4 + (z_hi + 1 + d // 3) % 4,
                x * 8 + ((z_lo + 1 + d % 3) % 4) * 2 + core,
            )
        )
        return carry

    def greet_plane(d, carry):
        to = (x * 2 + core + 1 + d % 7) % 8
        greet((((y + 1 + d // 7) % 4) * 4 + z_hi, (to // 2) * 8 + z_lo * 2 + to % 2))
        return carry

    loads = [
        pltpu.make_async_copy(source, dest, load_sem.at[at])
        for at, (source, dest) in enumerate(
            [
                (emb_hbm, emb_ref), (gain_hbm, gain_ref), (head_hbm, head_ref),
                (fwd_hbm, fwd_ref), (target_hbm, target_ref), (leg_hbm.at[s], leg_ref),
                (back_hbm, back_ref),
            ]
        )
    ]
    for load in loads:
        load.start()
    lax.fori_loop(0, MEMBERS - 1, greet_ens, 0, unroll=True)
    lax.fori_loop(0, 9, greet_z, 0, unroll=True)
    lax.fori_loop(0, SP - 1, greet_sp, 0, unroll=True)
    lax.fori_loop(0, 21, greet_plane, 0, unroll=True)

    lane = lax.broadcasted_iota(jnp.int32, (1, 128), 1)
    wide_lane = lax.broadcasted_iota(jnp.int32, (1, 256), 1)

    def turn(value, by):
        by = by % 128
        return pltpu.roll(value, by, 1) if by else value

    def grid_rows(row):
        at = 24 * row if row < 5 else 128
        return slice(at, at + 24)

    def to_waves():
        waves_ref[...] = three(dot_t, (fwd_ref[0], fwd_ref[1]), split(grid_ref[...]))

    def row_waves(row):
        group, start = (0, 24 * row) if row < 5 else (1, 0)
        parts = [
            turn(
                waves_ref[96 * hp : 96 * hp + 96, 128 * group : 128 * group + 128],
                24 * hp - start,
            )
            for hp in range(4)
        ]
        return jnp.where(
            lane < 48,
            jnp.where(lane < 24, parts[0], parts[1]),
            jnp.where(lane < 72, parts[2], parts[3]),
        )

    def every(row, block=0):
        return pl.ds(8 * block + row, SP, stride=16)

    def quarter(row, value):
        return turn(value, 32 * (row % 4) - 64)

    def pack(blocks, buffer):
        rest = [jnp.zeros((SP, 128), F32), jnp.zeros((SP, 128), F32)]
        for row in range(LOCAL_ROWS):
            first, second, third = blocks(row)
            buffer[every(row), :] = jnp.where(lane < 96, first, turn(third, 96))
            buffer[every(row, 1), :] = jnp.where(lane < 96, second, turn(third, 64))
            at = 32 * (row % 4)
            rest[row // 4] = jnp.where(
                (lane >= at) & (lane < at + 32), quarter(row, third), rest[row // 4]
            )
        buffer[every(6), :] = rest[0]
        buffer[every(7), :] = rest[1]

    def third_rows(buffer, row):
        return jnp.where(
            lane < 32,
            turn(buffer[every(row), :], 32),
            jnp.where(
                lane < 64,
                turn(buffer[every(row, 1), :], 64),
                turn(buffer[every(6 + row // 4), :], 64 - 32 * (row % 4)),
            ),
        )

    def exchange_sp(source, dest, at):
        size = source.shape[0] // SP

        def place(owner):
            return pl.ds(pl.multiple_of(size * owner, size), size)

        def send(n, carry):
            to, device = in_sp(n)
            pltpu.make_async_remote_copy(
                src_ref=source.at[place(to)],
                dst_ref=dest.at[place(s)],
                send_sem=send_sem.at[at], recv_sem=recv_sem.at[at],
                device_id=device, device_id_type=MESH,
            ).start()
            return carry

        lax.fori_loop(0, SP - 1, send, 0, unroll=True)
        dest[place(s), :] = source[place(s), :]

    def exchange_ens(source, dest, at):
        def send(n, carry):
            to, device = in_ens(n)
            pltpu.make_async_remote_copy(
                src_ref=source.at[to], dst_ref=dest.at[e],
                send_sem=send_sem.at[at], recv_sem=recv_sem.at[at],
                device_id=device, device_id_type=MESH,
            ).start()
            return carry

        lax.fori_loop(0, MEMBERS - 1, send, 0, unroll=True)
        dest[e] = source[e]

    def settle(piece, sem):
        pltpu.make_async_copy(piece, piece, sem).wait()

    def sp_piece(ref):
        return ref.at[pl.ds(0, ref.shape[0] // SP * (SP - 1))]

    def ens_piece(ref):
        return ref.at[pl.ds(0, MEMBERS - 1)]

    grid_ref[...] = jnp.zeros((256, COLS), F32)
    psend[...] = jnp.zeros((512, 128), F32)
    tsend[...] = jnp.zeros((256, 128), F32)
    third_ref[...] = jnp.zeros((256, 128), F32)
    for load in loads[:3]:
        load.wait()
    gain = gain_ref[...]
    head = head_ref[...]

    def norm_chunk(at, carry):
        rows = pl.ds(pl.multiple_of(at * STEP, STEP), STEP)
        xhat = standardize(emb_ref[rows, :].astype(F32))
        feat_ref[rows, 0:256] = (xhat * gain).astype(BF16)
        return carry

    lax.fori_loop(0, POINTS // STEP, norm_chunk, 0)
    for row in range(LOCAL_ROWS):
        grid_ref[grid_rows(row), :] = dot_t(head, feat_ref[COLS * row : COLS * row + COLS, 0:256])
    loads[3].wait()
    to_waves()

    def pred_blocks(row):
        block = row_waves(row)
        return [block[SP * i : SP * i + SP] for i in range(PAIRS)]

    pack(pred_blocks, psend)
    pl.semaphore_wait(barrier, SP - 1 + MEMBERS - 1 + 9 + 21)
    exchange_sp(psend, precv, 1)

    loads[4].wait()
    for row in range(LOCAL_ROWS):
        grid_ref[grid_rows(row), :] = target_ref[row].astype(F32)
    to_waves()
    column = (e % 3) * 16
    for row in range(LOCAL_ROWS):
        block = pltpu.roll(row_waves(row), (128 - column) % 128, 1)
        merged = jnp.zeros((SP, 128), F32)
        for i in range(PAIRS):
            part = block[SP * i : SP * i + SP]
            for h in range(2):
                at = 32 * i + 16 * h
                merged = jnp.where(
                    (lane >= at) & (lane < at + 16), turn(part, at - 48 * h), merged
                )
        tsend[pl.ds(row, SP, stride=8), :] = merged
    exchange_sp(tsend, trecv, 0)

    def xhat_chunk(at, carry):
        rows = pl.ds(pl.multiple_of(at * STEP, STEP), STEP)
        hi, lo = split(standardize(emb_ref[rows, :].astype(F32)))
        feat_ref[rows, 256:512] = hi
        feat_ref[rows, 512:768] = lo
        return carry

    lax.fori_loop(0, POINTS // STEP, xhat_chunk, 0)
    loads[5].wait()
    loads[6].wait()

    def edge(i):
        return MMAX - (SP * i + s)

    def terms_of(i, fields):
        return three(dot, (leg_ref[i, 0], leg_ref[i, 1]), split(fields)).T

    def tail_groups(tails):
        third = jnp.where(lane < 65, tails[0], pltpu.roll(tails[1], 65, 1))
        fourth = jnp.where(
            lane < 65, tails[2], jnp.where(lane < 67, pltpu.roll(tails[1], 2, 1), 0.0)
        )
        return third, fourth

    settle(sp_piece(precv), recv_sem.at[1])
    for row in range(LOCAL_ROWS):
        third_ref[pl.ds(row, SP, stride=8), :] = third_rows(precv, row)
    tails = []
    blocks = precv[...].reshape(SP, 2, 8, 128)
    for i, fields in enumerate(
        (blocks[:, 0].reshape(256, 128), blocks[:, 1].reshape(256, 128), third_ref[...])
    ):
        terms = terms_of(i, fields)
        packed = jnp.where(wide_lane < edge(i), terms[0:48], terms[48:96])
        for b in range(3):
            csend[3 * i + b] = packed[16 * b : 16 * b + 16, 0:128]
        tails.append(packed[:, 128:256])
    for c, group in enumerate(tail_groups(tails)):
        for b in range(3):
            csend[9 + 3 * c + b] = group[16 * b : 16 * b + 16]
    csend[15] = jnp.zeros((16, 128), F32)
    exchange_ens(csend, crecv, 2)

    settle(sp_piece(trecv), recv_sem.at[0])
    tails = []
    for i in range(PAIRS):
        terms = terms_of(i, trecv[...])
        packed = jnp.where(
            wide_lane < edge(i), terms[32 * i : 32 * i + 16], terms[32 * i + 16 : 32 * i + 32]
        )
        ctruth[i] = packed[:, 0:128]
        tails.append(packed[:, 128:256])
    ctruth[3], ctruth[4] = tail_groups(tails)
    ctruth[5] = jnp.zeros((16, 128), F32)
    truth = ctruth[e // 3]
    settle(ens_piece(crecv), recv_sem.at[2])

    members = crecv[...]

    def turned(value, by):
        by = by % MEMBERS
        return jnp.concatenate([value[MEMBERS - by :], value[: MEMBERS - by]], axis=0)

    pair = slope(members - turned(members, 8))
    for by in range(1, 8):
        term = slope(members - turned(members, by))
        pair = pair + (term - turned(term, -by))
    gsend[...] = slope(members - truth[None]) * (1.0 / (MEMBERS * LMAX)) - pair * (
        1.0 / (MEMBERS * (MEMBERS - 1) * LMAX)
    )
    exchange_ens(gsend, grecv, 3)
    settle(ens_piece(grecv), recv_sem.at[3])

    groups = [
        jnp.concatenate([grecv[3 * c + b] for b in range(3)], axis=0) for c in range(5)
    ]
    tails = [
        jnp.where(lane < 65, groups[3], 0.0),
        jnp.where(
            lane < 63,
            pltpu.roll(groups[3], 63, 1),
            jnp.where(lane < 65, pltpu.roll(groups[4], 126, 1), 0.0),
        ),
        jnp.where(lane < 65, groups[4], 0.0),
    ]
    for i in range(PAIRS):
        packed = jnp.concatenate([groups[i], tails[i]], axis=1)
        both = jnp.concatenate(
            [
                jnp.where(wide_lane < edge(i), packed, 0.0),
                jnp.where(wide_lane < edge(i), 0.0, packed),
                jnp.zeros((32, 256), F32),
            ],
            axis=0,
        )
        tall_ref[i] = three(dot, split(both), (leg_ref[i, 0], leg_ref[i, 1])).T
    bsend[...] = jnp.zeros((512, 128), F32)
    pack(lambda row: [tall_ref[i, pl.ds(row, SP, stride=8), :] for i in range(PAIRS)], bsend)
    exchange_sp(bsend, brecv, 4)
    settle(sp_piece(brecv), recv_sem.at[4])

    pieces = []
    for row in range(LOCAL_ROWS):
        block = jnp.concatenate(
            [
                brecv[every(row), :], brecv[every(row, 1), :], third_rows(brecv, row),
                jnp.zeros((32, 128), F32),
            ],
            axis=0,
        ).T
        pieces.append(
            jnp.concatenate([block[24 * hp : 24 * hp + 24] for hp in range(4)], axis=1)
        )
    waves = jnp.concatenate(pieces, axis=0)
    gpred = three(dot, split(waves), (back_ref[0], back_ref[1]))
    flat = jnp.concatenate(
        [gpred[24 * row : 24 * row + 24] for row in range(LOCAL_ROWS)], axis=1
    ).astype(BF16)
    grads = dot(flat, feat_ref[...])
    gain_grad = jnp.sum(
        (grads[:, 256:512] + grads[:, 512:768]) * head.astype(F32), axis=0, keepdims=True
    )
    for v in range(NVAR):
        rsend[v] = grads[v : v + 1, 0:256]
    rsend[NVAR] = gain_grad
    for r in range(NVAR + 1, 32):
        rsend[r] = jnp.zeros((1, 256), F32)

    def scatter(n, carry):
        to, device = in_plane(n)
        pltpu.make_async_remote_copy(
            src_ref=rsend.at[to], dst_ref=rrecv.at[plane],
            send_sem=send_sem.at[5], recv_sem=recv_sem.at[5],
            device_id=device, device_id_type=MESH,
        ).start()
        return carry

    lax.fori_loop(0, 31, scatter, 0, unroll=True)
    rrecv[plane] = rsend[plane]
    settle(rrecv.at[pl.ds(0, 31)], recv_sem.at[5])
    total = rrecv[0]
    for r in range(1, 32):
        total = total + rrecv[r]
    esend[...] = total

    def spread(n, carry):
        _, device = along_z(n)
        pltpu.make_async_remote_copy(
            src_ref=esend, dst_ref=erecv.at[z],
            send_sem=send_sem.at[6], recv_sem=recv_sem.at[6],
            device_id=device, device_id_type=MESH,
        ).start()
        return carry

    lax.fori_loop(0, 15, spread, 0, unroll=True)
    erecv[z] = total
    settle(erecv.at[pl.ds(0, 15)], recv_sem.at[6])
    total = erecv[0]
    for r in range(1, 16):
        total = total + erecv[r]
    sums_ref[plane] = total

    def gather(n, carry):
        _, device = in_plane(n)
        pltpu.make_async_remote_copy(
            src_ref=sums_ref.at[plane], dst_ref=sums_ref.at[plane],
            send_sem=send_sem.at[7], recv_sem=recv_sem.at[7],
            device_id=device, device_id_type=MESH,
        ).start()
        return carry

    lax.fori_loop(0, 31, gather, 0, unroll=True)
    settle(sp_piece(psend), send_sem.at[1])
    settle(sp_piece(tsend), send_sem.at[0])
    settle(ens_piece(csend), send_sem.at[2])
    settle(ens_piece(gsend), send_sem.at[3])
    settle(sp_piece(bsend), send_sem.at[4])
    settle(rsend.at[pl.ds(0, 31)], send_sem.at[5])
    settle(erecv.at[pl.ds(0, 15)], send_sem.at[6])
    settle(sums_ref.at[pl.ds(0, 31)], recv_sem.at[7])
    for v in range(NVAR):
        out_ref[v : v + 1, :] = sums_ref[v]
    out_gain_ref[...] = sums_ref[NVAR]
    settle(sums_ref.at[pl.ds(0, 31)], send_sem.at[7])


def per_device(forward, back, legendre, embedding, target, gain, head_w):
    vmem = pl.BlockSpec(memory_space=pltpu.VMEM)
    hbm = pl.BlockSpec(memory_space=pltpu.HBM)
    ens_block = pltpu.VMEM((MEMBERS, 16, 128), F32)
    two = pltpu.VMEM((512, 128), F32)
    one = pltpu.VMEM((256, 128), F32)
    rows = pltpu.VMEM((32, 1, 256), F32)
    grad_head, grad_gain = pl.pallas_call(
        kernel,
        out_shape=(
            jax.ShapeDtypeStruct((NVAR, EMBED), F32), jax.ShapeDtypeStruct((1, EMBED), F32),
        ),
        in_specs=[hbm] * 7,
        out_specs=(vmem, vmem),
        scratch_shapes=[
            pltpu.VMEM((POINTS, EMBED), BF16),
            pltpu.VMEM((LOCAL_ROWS, NVAR, COLS), BF16),
            pltpu.VMEM((1, EMBED), F32),
            pltpu.VMEM((NVAR, EMBED), BF16),
            pltpu.VMEM((2, 384, COLS), BF16),
            pltpu.VMEM((2, 512, COLS), BF16),
            pltpu.VMEM((PAIRS, 2, 256, 256), BF16),
            pltpu.VMEM((POINTS, 3 * EMBED), BF16),
            pltpu.VMEM((256, COLS), F32),
            pltpu.VMEM((384, 256), F32),
            pltpu.VMEM((256, 128), F32),
            pltpu.VMEM((PAIRS, 256, 128), F32),
            one, one, two, two,
            ens_block, ens_block, pltpu.VMEM((6, 16, 128), F32), ens_block, ens_block,
            two, two,
            rows, rows,
            pltpu.VMEM((1, 256), F32),
            pltpu.VMEM((16, 1, 256), F32),
            rows,
            pltpu.SemaphoreType.DMA((7,)),
            pltpu.SemaphoreType.DMA((8,)),
            pltpu.SemaphoreType.DMA((8,)),
        ],
        compiler_params=pltpu.CompilerParams(
            collective_id=0, has_side_effects=True, vmem_limit_bytes=63 * 1024 * 1024
        ),
        name="crps",
    )(
        embedding.reshape(POINTS, EMBED), jnp.swapaxes(target, 0, 1), gain.reshape(1, EMBED),
        head_w.T, forward, back, legendre,
    )
    grad_head, grad_gain = pl.pallas_call(
        copy_kernel,
        out_shape=(
            jax.ShapeDtypeStruct((NVAR, EMBED), F32), jax.ShapeDtypeStruct((1, EMBED), F32),
        ),
        in_specs=[hbm, hbm],
        out_specs=(hbm, hbm),
        scratch_shapes=[pltpu.SemaphoreType.DMA((2,))],
        compiler_params=pltpu.CompilerParams(vmem_limit_bytes=63 * 1024 * 1024),
        name="results",
    )(grad_head, grad_gain)
    return grad_head.T, grad_gain.reshape(EMBED)


def solution(mesh):
    forward, back = dft_tables()
    legendre = legendre_table()
    in_specs = (P("ens", "sp", None, None), P(None, "sp", None), P(), P())

    def run(*args):
        return jax.shard_map(
            functools.partial(
                per_device, jnp.asarray(forward), jnp.asarray(back), jnp.asarray(legendre)
            ),
            mesh=mesh, in_specs=in_specs, out_specs=(P(), P()), check_vma=False,
        )(*args)

    return run
```
